32 devices in a mesh: dp: 8 (over z, x), tensor: 4 (over y, core).
Axes of the slice: x: 2, y: 2, z: 4, core: 2. Of those that a mesh axis runs over, the one named last changes fastest.
Arguments:
- activations: bfloat16 [2, 32, 256, 4096], P(None, 'dp', None, 'tensor'), may hold values from -6 to 6
- out_grads: bfloat16 [2, 32, 256, 4096], P(None, 'dp', None, 'tensor'), may hold values from -6 to 6
- proj_in: bfloat16 [2, 4096, 64], P(None, 'tensor'), may hold values from -0.09375 to 0.09375
- proj_out: bfloat16 [2, 4096, 64], P(None, 'tensor'), may hold values from -0.09375 to 0.09375
- lengths: int32 [32], P('dp'), may hold values from 32 to 256, as said below
- test_feats: bfloat16 [2, 2048, 4096], P(None, 'dp'), may hold values from -0.0059814453 to 0.0059814453
- test_slot: int32 [2048], P('dp'), may hold values from 0 to 255, as said below
Outputs:
- scores: float32 [32, 1024], P('dp')
The draws below stay inside these ranges and needn't reach their ends.
Inputs may be any that keep to these rules, and one draw needn't show every extreme that they name: Positions from lengths[e] on are padding; some example has exactly 256 real tokens and some exactly 32. `test_slot`: within each aligned block of 256 test items a permutation of 0 to 255.
All inputs are finite; a program needn't handle non-finite values.
Results may differ from the reference program's by a relative error of at most 0.005.
Values may be sent and summed in bfloat16 or wider, within the bound.
A program may use at most 128 MiB of HBM per device.

```python
import jax
import jax.numpy as jnp
from jax import lax

D = 4096
RANK = 64
LAYERS = 2
STEPS = 4
EX_DEV = 4
SEQ = 256
TB = 256
FEAT = 4096
TRAIN = 32
TEST = 2048
N_DP = 8


def draw_lengths(key, part):
    first_key, second_key, third_key = jax.random.split(key, 3)
    drawn = jax.random.randint(first_key, (TRAIN,), SEQ // 8, SEQ + 1)
    longest = jax.random.randint(second_key, (), 0, TRAIN)
    shortest = (longest + 1 + jax.random.randint(third_key, (), 0, TRAIN - 1)) % TRAIN
    position = jnp.arange(TRAIN)
    drawn = jnp.where(position == longest, SEQ, drawn)
    drawn = jnp.where(position == shortest, SEQ // 8, drawn)
    return drawn.astype(jnp.int32)


def draw_test_slot(key, part):
    block_keys = jax.random.split(key, TEST // TB)
    orders = jax.vmap(lambda one_key: jax.random.permutation(one_key, TB))(block_keys)
    return orders.reshape(TEST).astype(jnp.int32)


def levels(rng, extent, cuts, least, largest):
    def one(dim, blocks):
        heights = jax.random.uniform(jax.random.fold_in(jax.random.fold_in(rng, 6), dim), (blocks,), jnp.float32, least / len(cuts), largest / len(cuts))
        return jnp.repeat(jnp.exp(heights), extent[dim] // blocks).reshape((-1,) + (1,) * (len(extent) - dim - 1))

    gain = one(*cuts[0])
    for cut in cuts[1:]:
        gain = gain * one(*cut)
    return gain


def scatter_about(key, extent, scale, bound, cuts=(), kind=jnp.bfloat16):
    factor_of = levels(key, extent, cuts, -0.22, 0.18) if cuts else 1.0
    values = jax.random.normal(key, extent, jnp.float32) * scale * factor_of
    return jnp.minimum(jnp.maximum(values, -bound), bound).astype(kind)


def setup_inputs(seed: int = 0) -> dict:
    seeds = jax.random.split(jax.random.key(seed), 8)
    return {
        "activations": scatter_about(seeds[0], (LAYERS, TRAIN, SEQ, D), 1.0, 6.0, ((1, 8), (3, 4))),
        "out_grads": scatter_about(seeds[1], (LAYERS, TRAIN, SEQ, D), 1.0, 6.0, ((1, 8), (3, 4))),
        "proj_in": scatter_about(seeds[2], (LAYERS, D, RANK), D ** -0.5, 0.09375, ((1, 4),)),
        "proj_out": scatter_about(seeds[3], (LAYERS, D, RANK), D ** -0.5, 0.09375, ((1, 4),)),
        "lengths": draw_lengths(jax.random.fold_in(seeds[7], 71), 0),
        "test_feats": scatter_about(seeds[5], (LAYERS, TEST, FEAT), 0.001, 0.0059814453, ((1, 8),)),
        "test_slot": draw_test_slot(jax.random.fold_in(seeds[7], 71), 0),
    }


def project(values, matrix):
    flat = jnp.dot(values.reshape(-1, D), matrix, preferred_element_type=jnp.float32)
    rounded = lax.optimization_barrier(flat.astype(jnp.bfloat16))
    return rounded.astype(jnp.float32).reshape(TRAIN, SEQ, RANK)


def reference(activations, out_grads, proj_in, proj_out, lengths, test_feats, test_slot):
    positions = jnp.arange(SEQ, dtype=jnp.int32)
    kept_mask = (positions[None, :] < lengths[:, None]).astype(jnp.float32)
    layer_feats = []
    for layer_index in range(LAYERS):
        act_proj = project(activations[layer_index], proj_in[layer_index])
        grad_proj = project(out_grads[layer_index], proj_out[layer_index]) * kept_mask[:, :, None]
        outer_sums = jnp.einsum("esa,esb->eab", grad_proj, act_proj, precision=lax.Precision.HIGHEST)
        layer_feats.append(outer_sums.reshape(TRAIN, FEAT).astype(jnp.bfloat16))
    features = jnp.concatenate(layer_feats, axis=1)
    test_flat = jnp.transpose(test_feats, (1, 0, 2)).reshape(TEST, LAYERS * FEAT)
    target = (jnp.arange(TEST, dtype=jnp.int32) // TB) * TB + test_slot
    ordered = jnp.zeros_like(test_flat).at[target].set(test_flat)
    all_scores = jnp.dot(features, ordered.T, preferred_element_type=jnp.float32)
    shard_of = jnp.arange(TRAIN, dtype=jnp.int32) // EX_DEV
    tile_index = jnp.arange(STEPS, dtype=jnp.int32)
    source = (shard_of[:, None] - tile_index[None, :]) % N_DP
    columns = source[:, :, None] * TB + jnp.arange(TB, dtype=jnp.int32)[None, None, :]
    columns = columns.reshape(TRAIN, STEPS * TB).astype(jnp.int32)
    return jnp.take_along_axis(all_scores, columns, axis=1)
```

```python
import functools

import jax
import jax.numpy as jnp
from jax import lax
from jax.experimental import pallas as pl
from jax.experimental.pallas import tpu as pltpu
from jax.sharding import PartitionSpec as P

STEPS = 4
LANES = 128
WIRE = jnp.float32
MESH = pl.DeviceIdType.MESH


def kernel(
    n_dp, n_t, examples, seq, plan,
    act, grad, win, wout, lens, tests, slot,
    out,
    abuf, gbuf, wpad, tbuf, ordered, msend, mrecv, own, ysend, yrecv,
    fscr, fsend, frecv, flat, ssend, srecv,
    in_sem, w_sem, t_sem, m_send, m_recv, y_send, y_recv, f_send, f_recv, s_send, s_recv,
):
    unit, n_unit, n_chip, rank = plan
    d, t = lax.axis_index("dp"), lax.axis_index("tensor")
    chip, core = t // 2, t % 2
    depth = act.shape[1]
    layer_rows = examples * seq
    rank_rows = rank * rank // LANES
    mate = {"dp": d, "tensor": 2 * chip + 1 - core}

    def row_of(chip_index, core_index, u):
        return ((2 * chip_index + core_index) * n_unit + u) * unit

    steps = [(o, u) for o in list(range(1, n_chip)) + [0] for u in range(n_unit)]
    units = []
    for o, u in steps:
        where = lax.rem(chip + o, n_chip)
        units.append(row_of(where, 1 - core, u))
        units.append(row_of(where, core, u))

    layers = win.shape[0]
    w_copies = []
    for layer in range(layers):
        w_copies.append(pltpu.make_async_copy(win.at[layer], wpad.at[layer, :rank, :depth], w_sem.at[2 * layer]))
        w_copies.append(pltpu.make_async_copy(wout.at[layer], wpad.at[layer, rank:, depth:], w_sem.at[2 * layer + 1]))
    in_copies = []
    for i, row in enumerate(units):
        rows = pl.ds(pl.multiple_of(row, unit), unit)
        in_copies.append((
            pltpu.make_async_copy(act.at[rows], abuf.at[i], in_sem.at[2 * i]),
            pltpu.make_async_copy(grad.at[rows], gbuf.at[i], in_sem.at[2 * i + 1]),
        ))
    my_row = row_of(chip, core, 0)
    my_layer = my_row // layer_rows
    t_copy = pltpu.make_async_copy(tests.at[my_layer], tbuf, t_sem)
    for copy in w_copies:
        copy.start()
    for pair in in_copies:
        pair[0].start()
        pair[1].start()
    t_copy.start()

    barrier = pltpu.get_barrier_semaphore()
    near = sorted({delta % n_dp for delta in range(1 - STEPS, STEPS)})
    for delta in near:
        for o in range(n_t):
            if delta or o:
                pl.semaphore_signal(
                    barrier, inc=1, device_id_type=MESH,
                    device_id={"dp": lax.rem(d + delta, n_dp), "tensor": lax.rem(t + o, n_t)},
                )

    empty = jnp.zeros((rank, depth), wpad.dtype)
    for layer in range(layers):
        wpad[layer, :rank, depth:] = empty
        wpad[layer, rank:, :depth] = empty
    for copy in w_copies:
        copy.wait()

    def project(i):
        for copy in in_copies[i]:
            copy.wait()
        layer = units[i] // layer_rows
        last = (((1,), (1,)), ((), ()))
        return lax.dot_general(
            abuf[i], wpad[layer, :, :depth], last, preferred_element_type=jnp.float32
        ) + lax.dot_general(gbuf[i], wpad[layer, :, depth:], last, preferred_element_type=jnp.float32)

    sends = []
    y_copies = {}
    for s, (o, u) in enumerate(steps):
        msend[s] = project(2 * s)
        if s == 0:
            pl.semaphore_wait(barrier, len(near) * n_t - 1)
        to_mate = pltpu.make_async_remote_copy(
            src_ref=msend.at[s], dst_ref=mrecv.at[s], send_sem=m_send.at[s], recv_sem=m_recv.at[s],
            device_id=mate, device_id_type=MESH,
        )
        to_mate.start()
        sends.append(to_mate)
        own[s] = project(2 * s + 1)
        to_mate.wait_recv()
        if o == 0:
            continue
        slot_of = (o - 1) * n_unit + u
        ysend[slot_of] = (own[s] + mrecv[s]).astype(ysend.dtype)
        across = pltpu.make_async_remote_copy(
            src_ref=ysend.at[slot_of], dst_ref=yrecv.at[slot_of],
            send_sem=y_send.at[slot_of], recv_sem=y_recv.at[slot_of],
            device_id={"dp": d, "tensor": 2 * lax.rem(chip + o, n_chip) + core}, device_id_type=MESH,
        )
        across.start()
        sends.append(across)
        y_copies[o, u] = across

    items = tbuf.shape[0]
    t_copy.wait()
    place = jnp.where(
        lax.broadcasted_iota(jnp.int32, (items, items), 0) == jnp.broadcast_to(slot[...], (items, items)), 1.0, 0.0
    ).astype(tbuf.dtype)
    wide = 2 * LANES

    def put(b, carry):
        columns = pl.ds(pl.multiple_of(b * wide, wide), wide)
        ordered[:, columns] = jnp.dot(place, tbuf[:, columns], preferred_element_type=jnp.float32).astype(ordered.dtype)
        return carry

    lax.fori_loop(0, tbuf.shape[1] // wide, put, 0)

    lane = lax.broadcasted_iota(jnp.int32, (unit, LANES), 1)
    token = lax.broadcasted_iota(jnp.int32, (unit, LANES), 0)
    lane_of = lax.broadcasted_iota(jnp.int32, (rank_rows, LANES), 1)
    for u in range(n_unit):
        s = (n_chip - 1) * n_unit + u
        total = own[s] + mrecv[s]
        for o in range(1, n_chip):
            y_copies[o, u].wait_recv()
            total = total + yrecv[(o - 1) * n_unit + u].astype(jnp.float32)
        row = row_of(chip, core, u)
        example = lax.rem(row, layer_rows) // seq
        kept = token + lax.rem(row, seq) < lens[example]
        total = jnp.where(kept, total, 0.0).astype(jnp.bfloat16).astype(jnp.float32)
        twice = jnp.where(lane < rank, total, pltpu.roll(total, rank, 1))
        outer = lax.dot_general(
            total.astype(jnp.bfloat16), twice.astype(jnp.bfloat16), (((0,), (0,)), ((), ())),
            preferred_element_type=jnp.float32,
        )
        fscr[u] = outer[rank:, :]
        even = fscr[u, pl.ds(0, rank_rows, stride=2), :]
        odd = fscr[u, pl.ds(1, rank_rows, stride=2), :]
        fsend[u] = jnp.where(lane_of < rank, even, odd).astype(jnp.bfloat16)

    feat_copies = []
    for r in range(1, STEPS):
        copy = pltpu.make_async_remote_copy(
            src_ref=fsend, dst_ref=frecv.at[r - 1], send_sem=f_send.at[r - 1], recv_sem=f_recv.at[r - 1],
            device_id={"dp": lax.rem(d + n_dp - r, n_dp), "tensor": t}, device_id_type=MESH,
        )
        copy.start()
        feat_copies.append(copy)
        sends.append(copy)

    filled = STEPS * n_unit * rank_rows
    rows = flat.shape[0] // rank_rows
    if flat.shape[0] > filled:
        flat[filled:, :] = jnp.zeros((flat.shape[0] - filled, LANES), jnp.float32)
    for r in range(STEPS):
        if r:
            feat_copies[r - 1].wait_recv()
        block = fsend[...] if r == 0 else frecv[r - 1]
        for u in range(n_unit):
            at = (r * n_unit + u) * rank_rows
            flat[at:at + rank_rows, :] = block[u].astype(jnp.float32)
    feats = jnp.concatenate(
        [flat[pl.ds(i, rows, stride=rank_rows), :] for i in range(rank_rows)], axis=1
    ).astype(jnp.bfloat16)
    scores = lax.dot_general(
        feats, ordered[...], (((1,), (1,)), ((), ())), preferred_element_type=jnp.float32
    )

    halves = items // LANES
    line = lax.broadcasted_iota(jnp.int32, (halves * examples, LANES), 0)
    back = []
    for r in [*range(1, STEPS), 0]:
        tile = jnp.zeros((halves * examples, LANES), jnp.float32)
        for u in range(n_unit):
            example = lax.rem(row_of(chip, core, u), layer_rows) // seq
            for h in range(halves):
                at = r * n_unit + u
                piece = scores[at:at + 1, h * LANES:(h + 1) * LANES]
                tile = jnp.where(line == example + h * examples, jnp.broadcast_to(piece, tile.shape), tile)
        ssend[r] = tile
        for o in range(n_t):
            if r == 0 and o == 0:
                continue
            at = r * n_t + o
            copy = pltpu.make_async_remote_copy(
                src_ref=ssend.at[r], dst_ref=srecv.at[at], send_sem=s_send.at[at], recv_sem=s_recv.at[at],
                device_id={"dp": lax.rem(d + r, n_dp), "tensor": lax.rem(t + o, n_t)}, device_id_type=MESH,
            )
            copy.start()
            back.append((at, copy))
    arrived = dict(back)
    for r in range(STEPS):
        tile = ssend[0] if r == 0 else jnp.zeros((halves * examples, LANES), jnp.float32)
        for o in range(n_t):
            at = r * n_t + o
            if at in arrived:
                arrived[at].wait_recv()
                tile = tile + srecv[at]
        for h in range(halves):
            start = r * items + h * LANES
            out[:, start:start + LANES] = tile[h * examples:(h + 1) * examples, :]
    for copy in sends:
        copy.wait_send()
    for at, copy in back:
        copy.wait_send()


def shards(n_dp, n_t, activations, out_grads, proj_in, proj_out, lengths, test_feats, test_slot):
    layers, examples, seq, depth = activations.shape
    rank = proj_in.shape[2]
    items, feat = test_feats.shape[1:]
    rows = layers * examples * seq
    chunk = rows // n_t
    unit = min(chunk, seq)
    n_unit = chunk // unit
    n_chip = n_t // 2
    n_step = n_chip * n_unit
    n_far = max(1, (n_chip - 1) * n_unit)
    rank_rows = rank * rank // LANES
    flat_rows = -(-STEPS * n_unit // 8) * 8
    tile_rows = items // LANES * examples
    dma = pltpu.SemaphoreType.DMA
    bf16, f32 = jnp.bfloat16, jnp.float32
    hbm = pl.BlockSpec(memory_space=pl.ANY)
    vmem = pl.BlockSpec(memory_space=pltpu.VMEM)
    call = pl.pallas_call(
        functools.partial(kernel, n_dp, n_t, examples, seq, (unit, n_unit, n_chip, rank)),
        out_shape=jax.ShapeDtypeStruct((examples, STEPS * items), f32),
        in_specs=[hbm, hbm, hbm, hbm, pl.BlockSpec(memory_space=pltpu.SMEM), hbm, vmem],
        out_specs=vmem,
        scratch_shapes=[
            pltpu.VMEM((2 * n_step, unit, depth), bf16),
            pltpu.VMEM((2 * n_step, unit, depth), bf16),
            pltpu.VMEM((layers, LANES, 2 * depth), bf16),
            pltpu.VMEM((items, feat), bf16),
            pltpu.VMEM((items, feat), bf16),
            pltpu.VMEM((n_step, unit, LANES), f32),
            pltpu.VMEM((n_step, unit, LANES), f32),
            pltpu.VMEM((n_step, unit, LANES), f32),
            pltpu.VMEM((n_far, unit, LANES), WIRE),
            pltpu.VMEM((n_far, unit, LANES), WIRE),
            pltpu.VMEM((n_unit, rank, LANES), f32),
            pltpu.VMEM((n_unit, rank_rows, LANES), bf16),
            pltpu.VMEM((STEPS - 1, n_unit, rank_rows, LANES), bf16),
            pltpu.VMEM((flat_rows * rank_rows, LANES), f32),
            pltpu.VMEM((STEPS, tile_rows, LANES), f32),
            pltpu.VMEM((STEPS * n_t, tile_rows, LANES), f32),
            dma((4 * n_step,)),
            dma((2 * layers,)),
            dma,
            dma((n_step,)),
            dma((n_step,)),
            dma((n_far,)),
            dma((n_far,)),
            dma((STEPS - 1,)),
            dma((STEPS - 1,)),
            dma((STEPS * n_t,)),
            dma((STEPS * n_t,)),
        ],
        compiler_params=pltpu.CompilerParams(
            collective_id=0, has_side_effects=True, vmem_limit_bytes=56 * 1024 * 1024
        ),
    )
    return call(
        activations.reshape(rows, depth),
        out_grads.reshape(rows, depth),
        proj_in.swapaxes(1, 2),
        proj_out.swapaxes(1, 2),
        lengths,
        test_feats,
        test_slot.reshape(1, items),
    )


def solution(mesh):
    return jax.shard_map(
        functools.partial(shards, mesh.shape["dp"], mesh.shape["tensor"]),
        mesh=mesh,
        in_specs=(
            P(None, "dp", None, "tensor"),
            P(None, "dp", None, "tensor"),
            P(None, "tensor", None),
            P(None, "tensor", None),
            P("dp"),
            P(None, "dp", None),
            P("dp"),
        ),
        out_specs=P("dp", None),
        check_vma=False,
    )
```

```python
import functools

import jax
import jax.numpy as jnp
from jax import lax
from jax.experimental import pallas as pl
from jax.experimental.pallas import tpu as pltpu
from jax.sharding import PartitionSpec as P

STEPS = 4
LANES = 128
WIRE = jnp.bfloat16
MESH = pl.DeviceIdType.MESH


def kernel(
    n_dp, n_t, examples, seq, plan,
    act, grad, win, wout, lens_hbm, tests, slot_hbm,
    out,
    lens, slot, l_sem,
    abuf, gbuf, wpad, tbuf, ordered, msend, mrecv, own, ysend, yrecv,
    fscr, fsend, frecv, flat, ssend, srecv,
    in_sem, w_sem, t_sem, m_send, m_recv, y_send, y_recv, f_send, f_recv, s_send, s_recv,
):
    unit, n_unit, n_chip, rank = plan
    d, t = lax.axis_index("dp"), lax.axis_index("tensor")
    chip, core = t // 2, t % 2
    depth = act.shape[1]
    layer_rows = examples * seq
    rank_rows = rank * rank // LANES
    mate = {"dp": d, "tensor": 2 * chip + 1 - core}

    def row_of(chip_index, core_index, u):
        return ((2 * chip_index + core_index) * n_unit + u) * unit

    steps = [(o, u) for o in list(range(1, n_chip)) + [0] for u in range(n_unit)]
    units = []
    for o, u in steps:
        where = lax.rem(chip + o, n_chip)
        units.append(row_of(where, 1 - core, u))
        units.append(row_of(where, core, u))

    layers = win.shape[0]
    w_copies = []
    for layer in range(layers):
        w_copies.append(pltpu.make_async_copy(win.at[layer], wpad.at[layer, :rank, :depth], w_sem.at[2 * layer]))
        w_copies.append(pltpu.make_async_copy(wout.at[layer], wpad.at[layer, rank:, depth:], w_sem.at[2 * layer + 1]))
    in_copies = []
    for i, row in enumerate(units):
        rows = pl.ds(pl.multiple_of(row, unit), unit)
        in_copies.append((
            pltpu.make_async_copy(act.at[rows], abuf.at[i], in_sem.at[2 * i]),
            pltpu.make_async_copy(grad.at[rows], gbuf.at[i], in_sem.at[2 * i + 1]),
        ))
    my_row = row_of(chip, core, 0)
    my_layer = my_row // layer_rows
    t_copy = pltpu.make_async_copy(tests.at[my_layer], tbuf, t_sem)
    for copy in w_copies:
        copy.start()
    for pair in in_copies:
        pair[0].start()
        pair[1].start()
    t_copy.start()
    l_copies = [pltpu.make_async_copy(lens_hbm, lens, l_sem.at[0]), pltpu.make_async_copy(slot_hbm, slot, l_sem.at[1])]
    for copy in l_copies:
        copy.start()

    barrier = pltpu.get_barrier_semaphore()
    near = sorted({delta % n_dp for delta in range(1 - STEPS, STEPS)})
    for delta in near:
        for o in range(n_t):
            if delta or o:
                pl.semaphore_signal(
                    barrier, inc=1, device_id_type=MESH,
                    device_id={"dp": lax.rem(d + delta, n_dp), "tensor": lax.rem(t + o, n_t)},
                )

    empty = jnp.zeros((rank, depth), wpad.dtype)
    for layer in range(layers):
        wpad[layer, :rank, depth:] = empty
        wpad[layer, rank:, :depth] = empty
    for copy in w_copies:
        copy.wait()

    def project(i):
        for copy in in_copies[i]:
            copy.wait()
        layer = units[i] // layer_rows
        last = (((1,), (1,)), ((), ()))
        return lax.dot_general(
            abuf[i], wpad[layer, :, :depth], last, preferred_element_type=jnp.float32
        ) + lax.dot_general(gbuf[i], wpad[layer, :, depth:], last, preferred_element_type=jnp.float32)

    sends = []
    y_copies = {}
    to_mates = []

    def pass_on(s):
        o, u = steps[s]
        if o == 0:
            return
        to_mates[s].wait_recv()
        at = (o - 1) * n_unit + u
        ysend[at] = (own[s] + mrecv[s]).astype(ysend.dtype)
        across = pltpu.make_async_remote_copy(
            src_ref=ysend.at[at], dst_ref=yrecv.at[at], send_sem=y_send.at[at], recv_sem=y_recv.at[at],
            device_id={"dp": d, "tensor": 2 * lax.rem(chip + o, n_chip) + core}, device_id_type=MESH,
        )
        across.start()
        sends.append(across)
        y_copies[o, u] = across

    for s in range(len(steps)):
        msend[s] = project(2 * s)
        if s == 0:
            pl.semaphore_wait(barrier, len(near) * n_t - 1)
        to_mate = pltpu.make_async_remote_copy(
            src_ref=msend.at[s], dst_ref=mrecv.at[s], send_sem=m_send.at[s], recv_sem=m_recv.at[s],
            device_id=mate, device_id_type=MESH,
        )
        to_mate.start()
        to_mates.append(to_mate)
        sends.append(to_mate)
        if s:
            pass_on(s - 1)
        own[s] = project(2 * s + 1)
    pass_on(len(steps) - 1)

    items = tbuf.shape[0]
    for copy in [t_copy, *l_copies]:
        copy.wait()
    place = jnp.where(
        lax.broadcasted_iota(jnp.int32, (items, items), 0) == jnp.broadcast_to(slot[...], (items, items)), 1.0, 0.0
    ).astype(tbuf.dtype)
    wide = 2 * LANES

    def put(b, carry):
        columns = pl.ds(pl.multiple_of(b * wide, wide), wide)
        ordered[:, columns] = jnp.dot(place, tbuf[:, columns], preferred_element_type=jnp.float32).astype(ordered.dtype)
        return carry

    lax.fori_loop(0, tbuf.shape[1] // wide, put, 0)

    lane = lax.broadcasted_iota(jnp.int32, (unit, LANES), 1)
    token = lax.broadcasted_iota(jnp.int32, (unit, LANES), 0)
    lane_of = lax.broadcasted_iota(jnp.int32, (rank_rows, LANES), 1)
    for u in range(n_unit):
        s = (n_chip - 1) * n_unit + u
        to_mates[s].wait_recv()
        total = own[s] + mrecv[s]
        for o in range(1, n_chip):
            y_copies[o, u].wait_recv()
            total = total + yrecv[(o - 1) * n_unit + u].astype(jnp.float32)
        row = row_of(chip, core, u)
        example = lax.rem(row, layer_rows) // seq
        kept = token + lax.rem(row, seq) < lens[example]
        total = jnp.where(kept, total, 0.0).astype(jnp.bfloat16).astype(jnp.float32)
        twice = jnp.where(lane < rank, total, pltpu.roll(total, rank, 1))
        outer = lax.dot_general(
            total.astype(jnp.bfloat16), twice.astype(jnp.bfloat16), (((0,), (0,)), ((), ())),
            preferred_element_type=jnp.float32,
        )
        fscr[u] = outer[rank:, :]
        even = fscr[u, pl.ds(0, rank_rows, stride=2), :]
        odd = fscr[u, pl.ds(1, rank_rows, stride=2), :]
        fsend[u] = jnp.where(lane_of < rank, even, odd).astype(jnp.bfloat16)

    feat_copies = []
    for r in range(1, STEPS):
        copy = pltpu.make_async_remote_copy(
            src_ref=fsend, dst_ref=frecv.at[r - 1], send_sem=f_send.at[r - 1], recv_sem=f_recv.at[r - 1],
            device_id={"dp": lax.rem(d + n_dp - r, n_dp), "tensor": t}, device_id_type=MESH,
        )
        copy.start()
        feat_copies.append(copy)
        sends.append(copy)

    filled = STEPS * n_unit * rank_rows
    rows = flat.shape[0] // rank_rows
    if flat.shape[0] > filled:
        flat[filled:, :] = jnp.zeros((flat.shape[0] - filled, LANES), jnp.float32)
    for r in range(STEPS):
        if r:
            feat_copies[r - 1].wait_recv()
        block = fsend[...] if r == 0 else frecv[r - 1]
        for u in range(n_unit):
            at = (r * n_unit + u) * rank_rows
            flat[at:at + rank_rows, :] = block[u].astype(jnp.float32)
    feats = jnp.concatenate(
        [flat[pl.ds(i, rows, stride=rank_rows), :] for i in range(rank_rows)], axis=1
    ).astype(jnp.bfloat16)
    scores = lax.dot_general(
        feats, ordered[...], (((1,), (1,)), ((), ())), preferred_element_type=jnp.float32
    )

    halves = items // LANES
    line = lax.broadcasted_iota(jnp.int32, (halves * examples, LANES), 0)
    back = []
    for r in [*range(1, STEPS), 0]:
        tile = jnp.zeros((halves * examples, LANES), jnp.float32)
        for u in range(n_unit):
            example = lax.rem(row_of(chip, core, u), layer_rows) // seq
            for h in range(halves):
                at = r * n_unit + u
                piece = scores[at:at + 1, h * LANES:(h + 1) * LANES]
                tile = jnp.where(line == example + h * examples, jnp.broadcast_to(piece, tile.shape), tile)
        ssend[r] = tile
        for o in range(n_t):
            if r == 0 and o == 0:
                continue
            at = r * n_t + o
            copy = pltpu.make_async_remote_copy(
                src_ref=ssend.at[r], dst_ref=srecv.at[at], send_sem=s_send.at[at], recv_sem=s_recv.at[at],
                device_id={"dp": lax.rem(d + r, n_dp), "tensor": lax.rem(t + o, n_t)}, device_id_type=MESH,
            )
            copy.start()
            back.append((at, copy))
    arrived = dict(back)
    for r in range(STEPS):
        tile = ssend[0] if r == 0 else jnp.zeros((halves * examples, LANES), jnp.float32)
        for o in range(n_t):
            at = r * n_t + o
            if at in arrived:
                arrived[at].wait_recv()
                tile = tile + srecv[at]
        for h in range(halves):
            start = r * items + h * LANES
            out[:, start:start + LANES] = tile[h * examples:(h + 1) * examples, :]
    for copy in sends:
        copy.wait_send()
    for at, copy in back:
        copy.wait_send()


def shards(n_dp, n_t, activations, out_grads, proj_in, proj_out, lengths, test_feats, test_slot):
    layers, examples, seq, depth = activations.shape
    rank = proj_in.shape[2]
    items, feat = test_feats.shape[1:]
    rows = layers * examples * seq
    chunk = rows // n_t
    unit = min(chunk, seq)
    n_unit = chunk // unit
    n_chip = n_t // 2
    n_step = n_chip * n_unit
    n_far = max(1, (n_chip - 1) * n_unit)
    rank_rows = rank * rank // LANES
    flat_rows = -(-STEPS * n_unit // 8) * 8
    tile_rows = items // LANES * examples
    dma = pltpu.SemaphoreType.DMA
    bf16, f32 = jnp.bfloat16, jnp.float32
    hbm = pl.BlockSpec(memory_space=pl.ANY)
    vmem = pl.BlockSpec(memory_space=pltpu.VMEM)
    call = pl.pallas_call(
        functools.partial(kernel, n_dp, n_t, examples, seq, (unit, n_unit, n_chip, rank)),
        out_shape=jax.ShapeDtypeStruct((examples, STEPS * items), f32),
        in_specs=[hbm] * 7,
        out_specs=vmem,
        scratch_shapes=[
            pltpu.SMEM((examples,), jnp.int32),
            pltpu.VMEM((1, items), jnp.int32),
            dma((2,)),
            pltpu.VMEM((2 * n_step, unit, depth), bf16),
            pltpu.VMEM((2 * n_step, unit, depth), bf16),
            pltpu.VMEM((layers, LANES, 2 * depth), bf16),
            pltpu.VMEM((items, feat), bf16),
            pltpu.VMEM((items, feat), bf16),
            pltpu.VMEM((n_step, unit, LANES), f32),
            pltpu.VMEM((n_step, unit, LANES), f32),
            pltpu.VMEM((n_step, unit, LANES), f32),
            pltpu.VMEM((n_far, unit, LANES), WIRE),
            pltpu.VMEM((n_far, unit, LANES), WIRE),
            pltpu.VMEM((n_unit, rank, LANES), f32),
            pltpu.VMEM((n_unit, rank_rows, LANES), bf16),
            pltpu.VMEM((STEPS - 1, n_unit, rank_rows, LANES), bf16),
            pltpu.VMEM((flat_rows * rank_rows, LANES), f32),
            pltpu.VMEM((STEPS, tile_rows, LANES), f32),
            pltpu.VMEM((STEPS * n_t, tile_rows, LANES), f32),
            dma((4 * n_step,)),
            dma((2 * layers,)),
            dma,
            dma((n_step,)),
            dma((n_step,)),
            dma((n_far,)),
            dma((n_far,)),
            dma((STEPS - 1,)),
            dma((STEPS - 1,)),
            dma((STEPS * n_t,)),
            dma((STEPS * n_t,)),
        ],
        compiler_params=pltpu.CompilerParams(
            collective_id=0, has_side_effects=True, vmem_limit_bytes=56 * 1024 * 1024
        ),
    )
    return call(
        activations.reshape(rows, depth),
        out_grads.reshape(rows, depth),
        proj_in.swapaxes(1, 2),
        proj_out.swapaxes(1, 2),
        lengths,
        test_feats,
        test_slot.reshape(1, items),
    )


def solution(mesh):
    return jax.shard_map(
        functools.partial(shards, mesh.shape["dp"], mesh.shape["tensor"]),
        mesh=mesh,
        in_specs=(
            P(None, "dp", None, "tensor"),
            P(None, "dp", None, "tensor"),
            P(None, "tensor", None),
            P(None, "tensor", None),
            P("dp"),
            P(None, "dp", None),
            P("dp"),
        ),
        out_specs=P("dp", None),
        check_vma=False,
    )
```

```python
import functools

import jax
import jax.numpy as jnp
from jax import lax
from jax.experimental import pallas as pl
from jax.experimental.pallas import tpu as pltpu
from jax.sharding import PartitionSpec as P

STEPS = 4
LANES = 128
WIRE = jnp.bfloat16
MESH = pl.DeviceIdType.MESH


def kernel(
    n_dp, n_t, examples, seq, plan,
    act, grad, win, wout, lens_hbm, tests, slot_hbm,
    out,
    lens, slot, l_sem,
    abuf, gbuf, wpad, wturn, tbuf, ordered, msend, mrecv, own, ysend, yrecv,
    fscr, fsend, frecv, flat, ssend, srecv,
    in_sem, w_sem, t_sem, m_send, m_recv, y_send, y_recv, f_send, f_recv, s_send, s_recv,
):
    unit, n_unit, n_chip, rank = plan
    d, t = lax.axis_index("dp"), lax.axis_index("tensor")
    chip, core = t // 2, t % 2
    depth = act.shape[1]
    layer_rows = examples * seq
    rank_rows = rank * rank // LANES
    mate = {"dp": d, "tensor": 2 * chip + 1 - core}

    def row_of(chip_index, core_index, u):
        return ((2 * chip_index + core_index) * n_unit + u) * unit

    steps = [(o, u) for o in list(range(1, n_chip)) + [0] for u in range(n_unit)]
    units = []
    for o, u in steps:
        where = lax.rem(chip + o, n_chip)
        units.append(row_of(where, 1 - core, u))
        units.append(row_of(where, core, u))

    layers = win.shape[0]
    w_copies = []
    for layer in range(layers):
        w_copies.append(pltpu.make_async_copy(win.at[layer], wpad.at[layer, :rank, :depth], w_sem.at[2 * layer]))
        w_copies.append(pltpu.make_async_copy(wout.at[layer], wpad.at[layer, rank:, depth:], w_sem.at[2 * layer + 1]))
    in_copies = []
    for i, row in enumerate(units):
        rows = pl.ds(pl.multiple_of(row, unit), unit)
        in_copies.append((
            pltpu.make_async_copy(act.at[rows], abuf.at[i], in_sem.at[2 * i]),
            pltpu.make_async_copy(grad.at[rows], gbuf.at[i], in_sem.at[2 * i + 1]),
        ))
    my_row = row_of(chip, core, 0)
    my_layer = my_row // layer_rows
    t_copy = pltpu.make_async_copy(tests.at[my_layer], tbuf, t_sem)
    for copy in w_copies:
        copy.start()
    for pair in in_copies:
        pair[0].start()
        pair[1].start()
    t_copy.start()
    l_copies = [pltpu.make_async_copy(lens_hbm, lens, l_sem.at[0]), pltpu.make_async_copy(slot_hbm, slot, l_sem.at[1])]
    for copy in l_copies:
        copy.start()

    barrier = pltpu.get_barrier_semaphore()
    near = sorted({delta % n_dp for delta in range(1 - STEPS, STEPS)})
    for delta in near:
        for o in range(n_t):
            if delta or o:
                pl.semaphore_signal(
                    barrier, inc=1, device_id_type=MESH,
                    device_id={"dp": lax.rem(d + delta, n_dp), "tensor": lax.rem(t + o, n_t)},
                )

    empty = jnp.zeros((rank, depth), wpad.dtype)
    for layer in range(layers):
        wpad[layer, :rank, depth:] = empty
        wpad[layer, rank:, :depth] = empty
    for copy in w_copies:
        copy.wait()
    for layer in range(layers):
        for b in range(2 * depth // LANES):
            part = slice(b * LANES, (b + 1) * LANES)
            wturn[layer, part, :] = wpad[layer, :, part].astype(jnp.float32).T.astype(wturn.dtype)

    def project(i):
        for copy in in_copies[i]:
            copy.wait()
        layer = units[i] // layer_rows
        return jnp.dot(abuf[i], wturn[layer, :depth, :], preferred_element_type=jnp.float32) + jnp.dot(
            gbuf[i], wturn[layer, depth:, :], preferred_element_type=jnp.float32
        )

    sends = []
    y_copies = {}
    to_mates = []

    def pass_on(s):
        o, u = steps[s]
        if o == 0:
            return
        to_mates[s].wait_recv()
        at = (o - 1) * n_unit + u
        ysend[at] = (own[s] + mrecv[s]).astype(ysend.dtype)
        across = pltpu.make_async_remote_copy(
            src_ref=ysend.at[at], dst_ref=yrecv.at[at], send_sem=y_send.at[at], recv_sem=y_recv.at[at],
            device_id={"dp": d, "tensor": 2 * lax.rem(chip + o, n_chip) + core}, device_id_type=MESH,
        )
        across.start()
        sends.append(across)
        y_copies[o, u] = across

    for s in range(len(steps)):
        msend[s] = project(2 * s)
        if s == 0:
            pl.semaphore_wait(barrier, len(near) * n_t - 1)
        to_mate = pltpu.make_async_remote_copy(
            src_ref=msend.at[s], dst_ref=mrecv.at[s], send_sem=m_send.at[s], recv_sem=m_recv.at[s],
            device_id=mate, device_id_type=MESH,
        )
        to_mate.start()
        to_mates.append(to_mate)
        sends.append(to_mate)
        if s:
            pass_on(s - 1)
        own[s] = project(2 * s + 1)
    pass_on(len(steps) - 1)

    items = tbuf.shape[0]
    for copy in [t_copy, *l_copies]:
        copy.wait()
    place = jnp.where(
        lax.broadcasted_iota(jnp.int32, (items, items), 0) == jnp.broadcast_to(slot[...], (items, items)), 1.0, 0.0
    ).astype(tbuf.dtype)
    wide = 2 * LANES

    def put(b, carry):
        columns = pl.ds(pl.multiple_of(b * wide, wide), wide)
        ordered[:, columns] = jnp.dot(place, tbuf[:, columns], preferred_element_type=jnp.float32).astype(ordered.dtype)
        return carry

    lax.fori_loop(0, tbuf.shape[1] // wide, put, 0)

    lane = lax.broadcasted_iota(jnp.int32, (unit, LANES), 1)
    token = lax.broadcasted_iota(jnp.int32, (unit, LANES), 0)
    lane_of = lax.broadcasted_iota(jnp.int32, (rank_rows, LANES), 1)
    for u in range(n_unit):
        s = (n_chip - 1) * n_unit + u
        to_mates[s].wait_recv()
        total = own[s] + mrecv[s]
        for o in range(1, n_chip):
            y_copies[o, u].wait_recv()
            total = total + yrecv[(o - 1) * n_unit + u].astype(jnp.float32)
        row = row_of(chip, core, u)
        example = lax.rem(row, layer_rows) // seq
        kept = token + lax.rem(row, seq) < lens[example]
        total = jnp.where(kept, total, 0.0).astype(jnp.bfloat16).astype(jnp.float32)
        twice = jnp.where(lane < rank, total, pltpu.roll(total, rank, 1))
        outer = lax.dot_general(
            total.astype(jnp.bfloat16), twice.astype(jnp.bfloat16), (((0,), (0,)), ((), ())),
            preferred_element_type=jnp.float32,
        )
        fscr[u] = outer[rank:, :]
        even = fscr[u, pl.ds(0, rank_rows, stride=2), :]
        odd = fscr[u, pl.ds(1, rank_rows, stride=2), :]
        fsend[u] = jnp.where(lane_of < rank, even, odd).astype(jnp.bfloat16)

    feat_copies = []
    for r in range(1, STEPS):
        copy = pltpu.make_async_remote_copy(
            src_ref=fsend, dst_ref=frecv.at[r - 1], send_sem=f_send.at[r - 1], recv_sem=f_recv.at[r - 1],
            device_id={"dp": lax.rem(d + n_dp - r, n_dp), "tensor": t}, device_id_type=MESH,
        )
        copy.start()
        feat_copies.append(copy)
        sends.append(copy)

    filled = STEPS * n_unit * rank_rows
    rows = flat.shape[0] // rank_rows
    if flat.shape[0] > filled:
        flat[filled:, :] = jnp.zeros((flat.shape[0] - filled, LANES), jnp.float32)
    for r in range(STEPS):
        if r:
            feat_copies[r - 1].wait_recv()
        block = fsend[...] if r == 0 else frecv[r - 1]
        for u in range(n_unit):
            at = (r * n_unit + u) * rank_rows
            flat[at:at + rank_rows, :] = block[u].astype(jnp.float32)
    feats = jnp.concatenate(
        [flat[pl.ds(i, rows, stride=rank_rows), :] for i in range(rank_rows)], axis=1
    ).astype(jnp.bfloat16)
    scores = lax.dot_general(
        feats, ordered[...], (((1,), (1,)), ((), ())), preferred_element_type=jnp.float32
    )

    halves = items // LANES
    line = lax.broadcasted_iota(jnp.int32, (halves * examples, LANES), 0)
    back = []
    for r in [*range(1, STEPS), 0]:
        tile = jnp.zeros((halves * examples, LANES), jnp.float32)
        for u in range(n_unit):
            example = lax.rem(row_of(chip, core, u), layer_rows) // seq
            for h in range(halves):
                at = r * n_unit + u
                piece = scores[at:at + 1, h * LANES:(h + 1) * LANES]
                tile = jnp.where(line == example + h * examples, jnp.broadcast_to(piece, tile.shape), tile)
        ssend[r] = tile
        for o in range(n_t):
            if r == 0 and o == 0:
                continue
            at = r * n_t + o
            copy = pltpu.make_async_remote_copy(
                src_ref=ssend.at[r], dst_ref=srecv.at[at], send_sem=s_send.at[at], recv_sem=s_recv.at[at],
                device_id={"dp": lax.rem(d + r, n_dp), "tensor": lax.rem(t + o, n_t)}, device_id_type=MESH,
            )
            copy.start()
            back.append((at, copy))
    arrived = dict(back)
    for r in range(STEPS):
        tile = ssend[0] if r == 0 else jnp.zeros((halves * examples, LANES), jnp.float32)
        for o in range(n_t):
            at = r * n_t + o
            if at in arrived:
                arrived[at].wait_recv()
                tile = tile + srecv[at]
        for h in range(halves):
            start = r * items + h * LANES
            out[:, start:start + LANES] = tile[h * examples:(h + 1) * examples, :]
    for copy in sends:
        copy.wait_send()
    for at, copy in back:
        copy.wait_send()


def shards(n_dp, n_t, activations, out_grads, proj_in, proj_out, lengths, test_feats, test_slot):
    layers, examples, seq, depth = activations.shape
    rank = proj_in.shape[2]
    items, feat = test_feats.shape[1:]
    rows = layers * examples * seq
    chunk = rows // n_t
    unit = min(chunk, seq)
    n_unit = chunk // unit
    n_chip = n_t // 2
    n_step = n_chip * n_unit
    n_far = max(1, (n_chip - 1) * n_unit)
    rank_rows = rank * rank // LANES
    flat_rows = -(-STEPS * n_unit // 8) * 8
    tile_rows = items // LANES * examples
    dma = pltpu.SemaphoreType.DMA
    bf16, f32 = jnp.bfloat16, jnp.float32
    hbm = pl.BlockSpec(memory_space=pl.ANY)
    vmem = pl.BlockSpec(memory_space=pltpu.VMEM)
    call = pl.pallas_call(
        functools.partial(kernel, n_dp, n_t, examples, seq, (unit, n_unit, n_chip, rank)),
        out_shape=jax.ShapeDtypeStruct((examples, STEPS * items), f32),
        in_specs=[hbm] * 7,
        out_specs=vmem,
        scratch_shapes=[
            pltpu.SMEM((examples,), jnp.int32),
            pltpu.VMEM((1, items), jnp.int32),
            dma((2,)),
            pltpu.VMEM((2 * n_step, unit, depth), bf16),
            pltpu.VMEM((2 * n_step, unit, depth), bf16),
            pltpu.VMEM((layers, LANES, 2 * depth), bf16),
            pltpu.VMEM((layers, 2 * depth, LANES), bf16),
            pltpu.VMEM((items, feat), bf16),
            pltpu.VMEM((items, feat), bf16),
            pltpu.VMEM((n_step, unit, LANES), f32),
            pltpu.VMEM((n_step, unit, LANES), f32),
            pltpu.VMEM((n_step, unit, LANES), f32),
            pltpu.VMEM((n_far, unit, LANES), WIRE),
            pltpu.VMEM((n_far, unit, LANES), WIRE),
            pltpu.VMEM((n_unit, rank, LANES), f32),
            pltpu.VMEM((n_unit, rank_rows, LANES), bf16),
            pltpu.VMEM((STEPS - 1, n_unit, rank_rows, LANES), bf16),
            pltpu.VMEM((flat_rows * rank_rows, LANES), f32),
            pltpu.VMEM((STEPS, tile_rows, LANES), f32),
            pltpu.VMEM((STEPS * n_t, tile_rows, LANES), f32),
            dma((4 * n_step,)),
            dma((2 * layers,)),
            dma,
            dma((n_step,)),
            dma((n_step,)),
            dma((n_far,)),
            dma((n_far,)),
            dma((STEPS - 1,)),
            dma((STEPS - 1,)),
            dma((STEPS * n_t,)),
            dma((STEPS * n_t,)),
        ],
        compiler_params=pltpu.CompilerParams(
            collective_id=0, has_side_effects=True, vmem_limit_bytes=56 * 1024 * 1024
        ),
    )
    return call(
        activations.reshape(rows, depth),
        out_grads.reshape(rows, depth),
        proj_in.swapaxes(1, 2),
        proj_out.swapaxes(1, 2),
        lengths,
        test_feats,
        test_slot.reshape(1, items),
    )


def solution(mesh):
    return jax.shard_map(
        functools.partial(shards, mesh.shape["dp"], mesh.shape["tensor"]),
        mesh=mesh,
        in_specs=(
            P(None, "dp", None, "tensor"),
            P(None, "dp", None, "tensor"),
            P(None, "tensor", None),
            P(None, "tensor", None),
            P("dp"),
            P(None, "dp", None),
            P("dp"),
        ),
        out_specs=P("dp", None),
        check_vma=False,
    )
```
